512 devices in a mesh: dp: 64 (over y, z), heads: 8 (over x, core).
Axes of the slice: x: 4, y: 4, z: 16, core: 2. Of those that a mesh axis runs over, the one named last changes fastest.
Arguments:
- queries: bfloat16 [64, 128, 8192], P('dp', 'heads'), may hold values from -14 to 14
- out_grad: bfloat16 [64, 128, 8192], P('dp', 'heads'), may hold values from -6 to 6
- keys: bfloat16 [64, 1792, 1024], P('dp', None, 'heads'), may hold values from -7 to 7
- values: bfloat16 [64, 1792, 1024], P('dp', None, 'heads'), may hold values from -4 to 4
- image_owner: int32 [64], replicated, may hold values from 0 to 63, each once
- tile_count: int32 [64], replicated, may hold values from 1 to 7, as said below
- seq_images: int32 [64, 2], replicated, may hold values from 0 to 63, as said below
- text_len: int32 [64], P('dp'), may hold values from 64 to 128, as said below
- tile_mask: int32 [64, 2, 7], P('dp'), may hold values from 0 to 1, as said below
Outputs:
- attn_out: bfloat16 [64, 128, 8192], P('dp', 'heads')
- query_grad: bfloat16 [64, 128, 8192], P('dp', 'heads')
- key_grad: bfloat16 [64, 1792, 1024], P('dp', None, 'heads')
- value_grad: bfloat16 [64, 1792, 1024], P('dp', None, 'heads')
The draws below stay inside these ranges and needn't reach their ends.
Inputs may be any that keep to these rules, and one draw needn't show every extreme that they name: `seq_images`: every image is read by at least one and at most 12 entries, and some image by exactly 12. A sequence may name one image twice. `tile_count`: some image has 7 tiles and some has 1. `text_len`: some sequence has 128 tokens and some 128 // 2. `tile_mask`: tile 0 of every image that a sequence reads is 1.
All inputs are finite; a program needn't handle non-finite values.
Results may differ from the reference program's by a relative error of at most 0.012.
Values may be sent and summed in bfloat16 or wider, within the bound.
A program may use at most 64 MiB of HBM per device.

```python
import math
import jax
import jax.numpy as jnp
from jax import lax

D_HEAD = 128
Q_HEADS = 64
KV_HEADS = 8
TILE = 256
TILES = 7
READS = 2
MOST_READ = 12
TEXT = 128
SEQS = 64
IMAGES = 64


def draw_queries(key, part):
    key = jax.random.fold_in(key, 3)
    key_noise = jax.random.fold_in(key, 0)
    noise_part = jnp.clip(jax.random.normal(key_noise, (SEQS, TEXT, Q_HEADS * D_HEAD), jnp.float32), -4.0, 4.0)
    return noise_part.astype(jnp.bfloat16)


def draw_keys(key, part):
    key = jax.random.fold_in(key, 4)
    noise_part = jnp.clip(jax.random.normal(key, (IMAGES, TILES * TILE, KV_HEADS * D_HEAD), jnp.float32), -4.0, 4.0)
    return noise_part.astype(jnp.bfloat16)


def draw_tile_count(key, part):
    key = jax.random.fold_in(key, 5)
    key_count, key_order = jax.random.split(key)
    counts = jax.random.randint(key_count, (IMAGES,), 1, TILES + 1)
    order_map = jax.random.permutation(key_order, IMAGES)
    counts = counts.at[order_map[0]].set(TILES).at[order_map[1]].set(1)
    return counts.astype(jnp.int32)


def draw_seq_images(key, part):
    key = jax.random.fold_in(key, 6)
    key_order, key_shuffle = jax.random.split(key)
    order_map = jax.random.permutation(key_order, IMAGES)
    total_reads = SEQS * READS
    read_index = jnp.arange(total_reads)
    picked = jnp.where(read_index < MOST_READ, 0, 1 + (read_index - MOST_READ) % (IMAGES - 1))
    read_list = order_map[picked]
    shuffled = read_list[jax.random.permutation(key_shuffle, total_reads)]
    return shuffled.reshape(SEQS, READS).astype(jnp.int32)


def draw_text_len(key, part):
    key = jax.random.fold_in(key, 7)
    key_len, key_order = jax.random.split(key)
    lengths = jax.random.randint(key_len, (SEQS,), TEXT // 2, TEXT + 1)
    order_map = jax.random.permutation(key_order, SEQS)
    lengths = lengths.at[order_map[0]].set(TEXT).at[order_map[1]].set(TEXT // 2)
    return lengths.astype(jnp.int32)


def draw_tile_mask(key, part):
    key = jax.random.fold_in(key, 8)
    flags = (jax.random.randint(key, (SEQS, READS, TILES), 0, 4) > 0).astype(jnp.int32)
    return flags.at[:, :, 0].set(1)


def level_of(own_key, shape, cuts, smallest, high):
    gain, own = 1.0, jax.random.fold_in(own_key, 6)
    for dim, shards_of in cuts:
        heights = jnp.exp(jax.random.uniform(jax.random.fold_in(own, dim), (shards_of,), jnp.float32, smallest / len(cuts), high / len(cuts)))
        gain = gain * jnp.repeat(heights, shape[dim] // shards_of).reshape([-1 if axis == dim else 1 for axis in range(len(shape))])
    return gain


def gaussian(rng, shape, spread, bound, cuts=(), held_as=jnp.bfloat16):
    values = jax.random.normal(rng, shape, jnp.float32) * spread
    if len(cuts) > 0:
        values = level_of(rng, shape, cuts, -0.22, 0.18) * values
    return jnp.clip(values, min=-bound, max=bound).astype(held_as)


def setup_inputs(seed: int = 0) -> dict:
    splits = jax.random.split(jax.random.key(seed), 10)
    queries = draw_queries(jax.random.fold_in(splits[9], 71), 0)
    out_grad = gaussian(splits[1], (SEQS, TEXT, Q_HEADS * D_HEAD), 1.0, 6.0, ((0, 64), (1, 8)))
    keys = draw_keys(jax.random.fold_in(splits[9], 71), 0)
    values = gaussian(splits[3], (IMAGES, TILES * TILE, KV_HEADS * D_HEAD), 1.0, 4.0, ((0, 64), (2, 8)))
    image_owner = jax.random.permutation(splits[4], IMAGES).astype(jnp.int32)
    tile_count = draw_tile_count(jax.random.fold_in(splits[9], 71), 0)
    seq_images = draw_seq_images(jax.random.fold_in(splits[9], 71), 0)
    text_len = draw_text_len(jax.random.fold_in(splits[9], 71), 0)
    tile_mask = draw_tile_mask(jax.random.fold_in(splits[9], 71), 0)
    return {"queries": queries, "out_grad": out_grad, "keys": keys, "values": values, "image_owner": image_owner, "tile_count": tile_count, "seq_images": seq_images, "text_len": text_len, "tile_mask": tile_mask}


def rounded(values_in):
    return lax.optimization_barrier(values_in.astype(jnp.bfloat16)).astype(jnp.float32)

def reference(queries, out_grad, keys, values, image_owner, tile_count, seq_images, text_len, tile_mask):
    group_size = Q_HEADS // KV_HEADS
    score_scale = 1.0 / math.sqrt(D_HEAD)
    key_rows = TILES * TILE
    highest = lax.Precision.HIGHEST
    image_ids = jnp.arange(IMAGES, dtype=jnp.int32)
    matches = seq_images[:, :, None] == image_ids[None, None, :]
    slot_of = lax.optimization_barrier(jnp.sum(jnp.where(matches, image_owner[None, None, :], 0), axis=2)).astype(jnp.int32)
    counts = lax.optimization_barrier(jnp.sum(jnp.where(matches, tile_count[None, None, :], 0), axis=2))
    tile_ok = (jnp.arange(TILES)[None, None, :] < counts[:, :, None]) & (tile_mask == 1)
    key_ok = jnp.repeat(tile_ok, TILE, axis=2)
    token_ok = (jnp.arange(TEXT)[None, :] < text_len[:, None]).astype(jnp.float32)

    def one_sequence(loop_state, inputs):
        key_acc, value_acc = loop_state
        query_seq, grad_seq, slots, key_mask, token_mask = inputs
        query_f = query_seq.astype(jnp.float32).reshape(TEXT, KV_HEADS, group_size, D_HEAD)
        key_f = keys[slots].astype(jnp.float32).reshape(READS, key_rows, KV_HEADS, D_HEAD)
        value_f = values[slots].astype(jnp.float32).reshape(READS, key_rows, KV_HEADS, D_HEAD)
        scores = jnp.einsum('tcge,jrce->jcgtr', query_f, key_f, precision=highest) * score_scale
        scores = jnp.where(key_mask[:, None, None, None, :], scores, -jnp.inf)
        peaks = lax.optimization_barrier(jnp.max(scores, axis=4, keepdims=True))
        expos = jnp.exp(scores - peaks)
        masses = lax.optimization_barrier(jnp.sum(expos, axis=4, keepdims=True))
        partial_out = jnp.einsum('jcgtr,jrce->jcgte', rounded(expos), value_f, precision=highest)
        top_peak = lax.optimization_barrier(jnp.max(peaks, axis=0))
        weights = jnp.exp(peaks - top_peak)
        total_mass = lax.optimization_barrier(jnp.sum(weights * masses, axis=0))
        row_mask = token_mask[None, None, :, None]
        mixture = lax.optimization_barrier(jnp.sum(weights * partial_out, axis=0)) / total_mass * row_mask
        log_mass = top_peak + jnp.log(total_mass)
        grad_in = grad_seq.astype(jnp.float32).reshape(TEXT, KV_HEADS, group_size, D_HEAD).transpose(1, 2, 0, 3) * row_mask
        deltas = lax.optimization_barrier(jnp.sum(grad_in * mixture, axis=3, keepdims=True))
        probs = jnp.exp(scores - log_mass[None])
        dprobs = jnp.einsum('cgte,jrce->jcgtr', grad_in, value_f, precision=highest)
        dscores = rounded(probs * (dprobs - deltas[None]) * score_scale)
        query_grad = jnp.einsum('jcgtr,jrce->tcge', dscores, key_f, precision=highest)
        key_part = rounded(jnp.einsum('jcgtr,tcge->jrce', dscores, query_f, precision=highest))
        value_part = rounded(jnp.einsum('jcgtr,cgte->jrce', rounded(probs), grad_in, precision=highest))
        key_acc = key_acc.at[slots].add(key_part.reshape(READS, key_rows, KV_HEADS * D_HEAD))
        value_acc = value_acc.at[slots].add(value_part.reshape(READS, key_rows, KV_HEADS * D_HEAD))
        attn_seq = mixture.transpose(2, 0, 1, 3).reshape(TEXT, Q_HEADS * D_HEAD).astype(jnp.bfloat16)
        grad_seq_out = query_grad.reshape(TEXT, Q_HEADS * D_HEAD).astype(jnp.bfloat16)
        return ((key_acc, value_acc), (attn_seq, grad_seq_out))
    zeros_acc = jnp.zeros((IMAGES, key_rows, KV_HEADS * D_HEAD), jnp.float32)
    (key_total, value_total), (attn_out, query_grad) = lax.scan(one_sequence, (zeros_acc, zeros_acc), (queries, out_grad, slot_of, key_ok, token_ok))
    return (attn_out, query_grad, key_total.astype(jnp.bfloat16), value_total.astype(jnp.bfloat16))
```

```python
import functools
import math

import jax
import jax.numpy as jnp
from jax import lax
from jax.experimental import pallas as pl
from jax.experimental.pallas import tpu as pltpu
from jax.sharding import PartitionSpec as P

D_HEAD = 128
NY = 4
NZ = 16
NH = 8
TILES = 7
READS = 2
BLOCK = 16
TEXT = 128
GROUP = 8
ROWS = TEXT * GROUP
WIDTH = GROUP * D_HEAD
SLOTS = NY * NZ
UNITS = READS * TILES
MESH = pl.DeviceIdType.MESH
VMEM_BYTES = 56 * 1024 * 1024


def far_first(step):
    half = step // 2
    return jnp.where(lax.rem(step, 2) == 1, 8 + half, 8 - half)


def place():
    me = lax.axis_index("dp")
    return me, me // NZ, lax.rem(me, NZ), lax.axis_index("heads")


def greet_all():
    me, my, mz, mh = place()
    barrier = pltpu.get_barrier_semaphore()

    def greet(device):
        pl.semaphore_signal(barrier, inc=1, device_id=device, device_id_type=MESH)

    def greet_z(step, carry):
        greet((my * NZ + lax.rem(mz + step, NZ), mh))
        return carry

    def greet_y(step, carry):
        greet((lax.rem(my + step, NY) * NZ + mz, mh))
        return carry

    def greet_h(step, carry):
        greet((me, lax.rem(mh + step, NH)))
        return carry

    lax.fori_loop(1, NZ, greet_z, 0)
    lax.fori_loop(1, NY, greet_y, 0)
    lax.fori_loop(1, NH, greet_h, 0)
    pl.semaphore_wait(barrier, NZ + NY + NH - 3)


def loop(start, stop, step_of):
    def body(step, carry):
        step_of(step)
        return carry

    lax.fori_loop(start, stop, body, 0)


def fetch_kernel(
    slots, q, g, k, v, q_out, g_out, k_out, v_out,
    held_k, held_v, send_k, send_v,
    head_send, head_recv, a_send, a_recv, b_send, b_recv, c_send, c_recv, local_sem,
):
    me, my, mz, mh = place()
    greet_all()
    sides = ((k, held_k, send_k, k_out), (v, held_v, send_v, v_out))

    def scatter(side, step):
        to = lax.rem(mz + far_first(step), NZ)
        return pltpu.make_async_remote_copy(
            src_ref=sides[side][0].at[:, to],
            dst_ref=sides[side][1].at[me],
            send_sem=a_send.at[side, to],
            recv_sem=a_recv.at[side, mz],
            device_id=(my * NZ + to, mh),
            device_id_type=MESH,
        )

    def scattered(side, source):
        return pltpu.make_async_remote_copy(
            src_ref=sides[side][0].at[:, source],
            dst_ref=sides[side][1].at[my * NZ + source],
            send_sem=a_send.at[side, source],
            recv_sem=a_recv.at[side, source],
            device_id=(my * NZ + source, mh),
            device_id_type=MESH,
        )

    def keep(side):
        return pltpu.make_async_copy(
            sides[side][0].at[:, mz], sides[side][1].at[me], local_sem.at[side]
        )

    def exchange(which, step):
        src, dst = ((q, q_out), (g, g_out))[which]
        to = lax.rem(mh + step, NH)
        return pltpu.make_async_remote_copy(
            src_ref=src.at[:, pl.ds(pl.multiple_of(to * WIDTH, WIDTH), WIDTH)],
            dst_ref=dst.at[mh],
            send_sem=head_send.at[which, to],
            recv_sem=head_recv.at[which, mh],
            device_id=(me, to),
            device_id_type=MESH,
        )

    def exchanged(which, step):
        src, dst = ((q, q_out), (g, g_out))[which]
        source = lax.rem(mh + step, NH)
        return pltpu.make_async_remote_copy(
            src_ref=src.at[:, pl.ds(pl.multiple_of(source * WIDTH, WIDTH), WIDTH)],
            dst_ref=dst.at[source],
            send_sem=head_send.at[which, source],
            recv_sem=head_recv.at[which, source],
            device_id=(me, source),
            device_id_type=MESH,
        )

    def own(which):
        src, dst = ((q, q_out), (g, g_out))[which]
        return pltpu.make_async_copy(
            src.at[:, pl.ds(pl.multiple_of(mh * WIDTH, WIDTH), WIDTH)],
            dst.at[mh],
            local_sem.at[2 + which],
        )

    def share(side, source, step):
        to = lax.rem(my + step, NY)
        return pltpu.make_async_remote_copy(
            src_ref=sides[side][1].at[my * NZ + source],
            dst_ref=sides[side][1].at[my * NZ + source],
            send_sem=b_send.at[side, to, source],
            recv_sem=b_recv.at[side, my, source],
            device_id=(to * NZ + mz, mh),
            device_id_type=MESH,
        )

    def shared(side, source, step):
        origin = lax.rem(my + step, NY)
        return pltpu.make_async_remote_copy(
            src_ref=sides[side][1].at[origin * NZ + source],
            dst_ref=sides[side][1].at[origin * NZ + source],
            send_sem=b_send.at[side, origin, source],
            recv_sem=b_recv.at[side, origin, source],
            device_id=(origin * NZ + mz, mh),
            device_id_type=MESH,
        )

    def deliver(side, to):
        return pltpu.make_async_remote_copy(
            src_ref=sides[side][2].at[to],
            dst_ref=sides[side][3].at[mz],
            send_sem=c_send.at[side, to],
            recv_sem=c_recv.at[side, mz],
            device_id=(my * NZ + to, mh),
            device_id_type=MESH,
        )

    def delivered(side, source):
        return pltpu.make_async_remote_copy(
            src_ref=sides[side][2].at[source],
            dst_ref=sides[side][3].at[source],
            send_sem=c_send.at[side, source],
            recv_sem=c_recv.at[side, source],
            device_id=(my * NZ + source, mh),
            device_id_type=MESH,
        )

    def deliver_own(side):
        return pltpu.make_async_copy(
            sides[side][2].at[mz], sides[side][3].at[mz], local_sem.at[4 + side]
        )

    for side in range(2):
        keep(side).start()
        loop(1, NZ, lambda step: scatter(side, step).start())
    for which in range(2):
        own(which).start()
        loop(1, NH, lambda step: exchange(which, step).start())

    def pass_on(side):
        keep(side).wait()
        loop(1, NY, lambda step: share(side, mz, step).start())

        def forward(step):
            source = lax.rem(mz + far_first(step), NZ)
            scattered(side, source).wait_recv()
            loop(1, NY, lambda turn: share(side, source, turn).start())

        loop(1, NZ, forward)

    def send_reads(side):
        held, send = sides[side][1], sides[side][2]
        loop(1, NY, lambda turn: loop(0, NZ, lambda source: shared(side, source, turn).wait_recv()))

        def gather(to):
            for read in range(READS):
                slot = slots[(my * NZ + to) * READS + read]
                send[to, read] = held[slot]

        def one(step):
            to = lax.rem(mz + far_first(step), NZ)
            gather(to)
            deliver(side, to).start()

        loop(1, NZ, one)
        gather(mz)
        deliver_own(side).start()

    pass_on(0)
    send_reads(0)
    pass_on(1)
    send_reads(1)

    for which in range(2):
        own(which).wait()
        loop(1, NH, lambda step: exchanged(which, step).wait_recv())
        loop(1, NH, lambda step: exchange(which, step).wait_send())
    for side in range(2):
        deliver_own(side).wait()
        loop(1, NZ, lambda step: scatter(side, step).wait_send())
        loop(1, NY, lambda turn: loop(0, NZ, lambda source: share(side, source, turn).wait_send()))
        loop(1, NZ, lambda step: delivered(side, lax.rem(mz + step, NZ)).wait_recv())
        loop(1, NZ, lambda step: deliver(side, lax.rem(mz + step, NZ)).wait_send())


def fetch(slots, q, g, k, v):
    any_spec = pl.BlockSpec(memory_space=pl.ANY)
    part = (TILES, BLOCK, D_HEAD)
    dma = pltpu.SemaphoreType.DMA
    return pl.pallas_call(
        fetch_kernel,
        out_shape=(
            jax.ShapeDtypeStruct((NH, TEXT // NH, WIDTH), jnp.bfloat16),
            jax.ShapeDtypeStruct((NH, TEXT // NH, WIDTH), jnp.bfloat16),
            jax.ShapeDtypeStruct((NZ, READS) + part, jnp.bfloat16),
            jax.ShapeDtypeStruct((NZ, READS) + part, jnp.bfloat16),
        ),
        in_specs=[pl.BlockSpec(memory_space=pltpu.SMEM)] + [any_spec] * 4,
        out_specs=(any_spec,) * 4,
        scratch_shapes=[
            pltpu.VMEM((SLOTS,) + part, jnp.bfloat16),
            pltpu.VMEM((SLOTS,) + part, jnp.bfloat16),
            pltpu.VMEM((NZ, READS) + part, jnp.bfloat16),
            pltpu.VMEM((NZ, READS) + part, jnp.bfloat16),
            dma((2, NH)), dma((2, NH)),
            dma((2, NZ)), dma((2, NZ)),
            dma((2, NY, NZ)), dma((2, NY, NZ)),
            dma((2, NZ)), dma((2, NZ)),
            dma((6,)),
        ],
        compiler_params=pltpu.CompilerParams(
            collective_id=1, has_side_effects=True, vmem_limit_bytes=VMEM_BYTES
        ),
        name="fetch",
    )(slots, q, g, k, v)


def attend_kernel(
    order, facts, q, g, k, v, attn, q_grad, k_grad, v_grad,
    q_rows, g_rows, q_cols, g_cols, scores,
):
    active = facts[0]
    length = facts[1]
    scale = 1.0 / math.sqrt(D_HEAD)
    token = lax.broadcasted_iota(jnp.int32, (TEXT, D_HEAD), 0)
    for head in range(GROUP):
        lanes = slice(head * D_HEAD, (head + 1) * D_HEAD)
        rows = slice(head * TEXT, (head + 1) * TEXT)
        q_head = q[:, lanes]
        g_head = jnp.where(token < length, g[:, lanes].astype(jnp.float32), 0.0)
        q_rows[rows, :] = q_head
        g_rows[rows, :] = g_head.astype(jnp.bfloat16)
        q_cols[:, rows] = jnp.transpose(q_head.astype(jnp.float32)).astype(jnp.bfloat16)
        g_cols[:, rows] = jnp.transpose(g_head).astype(jnp.bfloat16)

    def tile_of(ref, unit):
        return ref[:, unit].reshape(NZ * BLOCK, D_HEAD)

    def nn(left, right):
        return jnp.dot(left, right, preferred_element_type=jnp.float32)

    def tn(left, right):
        return lax.dot_general(
            left, right, (((0,), (0,)), ((), ())), preferred_element_type=jnp.float32
        )

    def score_step(index, peak):
        unit = order[index]
        part = nn(tile_of(k, unit), q_cols[...])
        scores[unit] = part
        return jnp.maximum(peak, jnp.max(part, axis=0, keepdims=True))

    peak = lax.fori_loop(
        0, active, score_step, jnp.full((1, ROWS), -jnp.inf, jnp.float32)
    )
    peak_scaled = peak * scale

    def mix_step(index, state):
        mass, mixed = state
        unit = order[index]
        expo = jnp.exp(scores[unit] * scale - peak_scaled)
        scores[unit] = expo
        mass = mass + jnp.sum(expo, axis=0, keepdims=True)
        mixed = mixed + tn(tile_of(v, unit), expo.astype(jnp.bfloat16))
        return mass, mixed

    mass, mixed = lax.fori_loop(
        0,
        active,
        mix_step,
        (jnp.zeros((1, ROWS), jnp.float32), jnp.zeros((D_HEAD, ROWS), jnp.float32)),
    )
    inverse = 1.0 / mass
    column = lax.rem(lax.broadcasted_iota(jnp.int32, (1, ROWS), 1), TEXT)
    mixture = mixed * jnp.where(column < length, inverse, 0.0)
    delta = jnp.sum(mixture * g_cols[...].astype(jnp.float32), axis=0, keepdims=True)
    for head in range(GROUP):
        lanes = slice(head * D_HEAD, (head + 1) * D_HEAD)
        attn[:, lanes] = jnp.transpose(mixture[:, lanes]).astype(jnp.bfloat16)

    def back_step(index, q_total):
        unit = order[index]
        probs = scores[unit] * inverse
        v_grad[:, unit] = (
            nn(probs.astype(jnp.bfloat16), g_rows[...])
            .astype(jnp.bfloat16)
            .reshape(NZ, BLOCK, D_HEAD)
        )
        inner = nn(tile_of(v, unit), g_cols[...])
        dscores = (probs * ((inner - delta) * scale)).astype(jnp.bfloat16)
        k_grad[:, unit] = (
            nn(dscores, q_rows[...]).astype(jnp.bfloat16).reshape(NZ, BLOCK, D_HEAD)
        )
        return q_total + tn(tile_of(k, unit), dscores)

    q_total = lax.fori_loop(0, active, back_step, jnp.zeros((D_HEAD, ROWS), jnp.float32))
    for head in range(GROUP):
        lanes = slice(head * D_HEAD, (head + 1) * D_HEAD)
        q_grad[:, lanes] = jnp.transpose(q_total[:, lanes]).astype(jnp.bfloat16)

    def clear_step(index, carry):
        unit = order[index]
        nothing = jnp.zeros((NZ, BLOCK, D_HEAD), jnp.bfloat16)
        k_grad[:, unit] = nothing
        v_grad[:, unit] = nothing
        return carry

    lax.fori_loop(active, UNITS, clear_step, 0)


def attend(order, facts, q, g, k, v):
    smem = pl.BlockSpec(memory_space=pltpu.SMEM)
    vmem = pl.BlockSpec(memory_space=pltpu.VMEM)
    reads = (NZ, UNITS, BLOCK, D_HEAD)
    return pl.pallas_call(
        attend_kernel,
        out_shape=(
            jax.ShapeDtypeStruct((TEXT, WIDTH), jnp.bfloat16),
            jax.ShapeDtypeStruct((TEXT, WIDTH), jnp.bfloat16),
            jax.ShapeDtypeStruct(reads, jnp.bfloat16),
            jax.ShapeDtypeStruct(reads, jnp.bfloat16),
        ),
        in_specs=[smem, smem] + [vmem] * 4,
        out_specs=(vmem,) * 4,
        scratch_shapes=[
            pltpu.VMEM((ROWS, D_HEAD), jnp.bfloat16),
            pltpu.VMEM((ROWS, D_HEAD), jnp.bfloat16),
            pltpu.VMEM((D_HEAD, ROWS), jnp.bfloat16),
            pltpu.VMEM((D_HEAD, ROWS), jnp.bfloat16),
            pltpu.VMEM((UNITS, NZ * BLOCK, ROWS), jnp.float32),
        ],
        compiler_params=pltpu.CompilerParams(vmem_limit_bytes=VMEM_BYTES),
        name="attend",
    )(order, facts, q.reshape(TEXT, WIDTH), g.reshape(TEXT, WIDTH), k.reshape(reads), v.reshape(reads))


def give_kernel(
    order, same, last, has, attn, q_grad, k_part, v_part,
    attn_out, q_out, k_out, v_out,
    back_k, back_v, run, row_k, row_v, col_k, col_v, sum_k, sum_v,
    head_send, head_recv, a_send, a_recv, b_send, b_recv, c_send, c_recv, local_sem,
):
    me, my, mz, mh = place()
    greet_all()
    sides = (
        (v_part, back_v, row_v, col_v, sum_v, v_out),
        (k_part, back_k, row_k, col_k, sum_k, k_out),
    )

    def give(side, to):
        return pltpu.make_async_remote_copy(
            src_ref=sides[side][0].at[pl.ds(to * READS, READS)],
            dst_ref=sides[side][1].at[pl.ds(mz * READS, READS)],
            send_sem=c_send.at[side, to],
            recv_sem=c_recv.at[side, mz],
            device_id=(my * NZ + to, mh),
            device_id_type=MESH,
        )

    def given(side, source):
        return pltpu.make_async_remote_copy(
            src_ref=sides[side][0].at[pl.ds(source * READS, READS)],
            dst_ref=sides[side][1].at[pl.ds(source * READS, READS)],
            send_sem=c_send.at[side, source],
            recv_sem=c_recv.at[side, source],
            device_id=(my * NZ + source, mh),
            device_id_type=MESH,
        )

    def give_own(side):
        return pltpu.make_async_copy(
            sides[side][0].at[pl.ds(mz * READS, READS)],
            sides[side][1].at[pl.ds(mz * READS, READS)],
            local_sem.at[side],
        )

    def exchange(which, to):
        src, dst = ((attn, attn_out), (q_grad, q_out))[which]
        return pltpu.make_async_remote_copy(
            src_ref=src.at[to],
            dst_ref=dst.at[:, pl.ds(pl.multiple_of(mh * WIDTH, WIDTH), WIDTH)],
            send_sem=head_send.at[which, to],
            recv_sem=head_recv.at[which, mh],
            device_id=(me, to),
            device_id_type=MESH,
        )

    def exchanged(which, source):
        src, dst = ((attn, attn_out), (q_grad, q_out))[which]
        return pltpu.make_async_remote_copy(
            src_ref=src.at[source],
            dst_ref=dst.at[:, pl.ds(pl.multiple_of(source * WIDTH, WIDTH), WIDTH)],
            send_sem=head_send.at[which, source],
            recv_sem=head_recv.at[which, source],
            device_id=(me, source),
            device_id_type=MESH,
        )

    def own(which):
        src, dst = ((attn, attn_out), (q_grad, q_out))[which]
        return pltpu.make_async_copy(
            src.at[mh],
            dst.at[:, pl.ds(pl.multiple_of(mh * WIDTH, WIDTH), WIDTH)],
            local_sem.at[2 + which],
        )

    def hand(side, step):
        to = lax.rem(my + step, NY)
        return pltpu.make_async_remote_copy(
            src_ref=sides[side][2].at[pl.ds(to * NZ, NZ)],
            dst_ref=sides[side][3].at[my],
            send_sem=b_send.at[side, to],
            recv_sem=b_recv.at[side, my],
            device_id=(to * NZ + mz, mh),
            device_id_type=MESH,
        )

    def handed(side, step):
        source = lax.rem(my + step, NY)
        return pltpu.make_async_remote_copy(
            src_ref=sides[side][2].at[pl.ds(source * NZ, NZ)],
            dst_ref=sides[side][3].at[source],
            send_sem=b_send.at[side, source],
            recv_sem=b_recv.at[side, source],
            device_id=(source * NZ + mz, mh),
            device_id_type=MESH,
        )

    def bring(side, to):
        return pltpu.make_async_remote_copy(
            src_ref=sides[side][4].at[to],
            dst_ref=sides[side][5].at[:, mz],
            send_sem=a_send.at[side, to],
            recv_sem=a_recv.at[side, mz],
            device_id=(my * NZ + to, mh),
            device_id_type=MESH,
        )

    def brought(side, source):
        return pltpu.make_async_remote_copy(
            src_ref=sides[side][4].at[source],
            dst_ref=sides[side][5].at[:, source],
            send_sem=a_send.at[side, source],
            recv_sem=a_recv.at[side, source],
            device_id=(my * NZ + source, mh),
            device_id_type=MESH,
        )

    def bring_own(side):
        return pltpu.make_async_copy(
            sides[side][4].at[mz], sides[side][5].at[:, mz], local_sem.at[4 + side]
        )

    for side in range(2):
        give_own(side).start()
        loop(1, NZ, lambda step: give(side, lax.rem(mz + far_first(step), NZ)).start())
    for which in range(2):
        own(which).start()
        loop(1, NH, lambda step: exchange(which, lax.rem(mh + step, NH)).start())

    def sum_reads(side):
        back, row = sides[side][1], sides[side][2]
        give_own(side).wait()
        loop(1, NZ, lambda step: given(side, lax.rem(mz + step, NZ)).wait_recv())
        run[0] = back[order[0]].astype(jnp.float32)

        def add(step):
            weight = same[step].astype(jnp.float32)
            run[step] = run[step - 1] * weight + back[order[step]].astype(jnp.float32)

        loop(1, NZ * READS, add)

        def pick(slot):
            weight = has[slot].astype(jnp.float32)
            row[slot] = (run[last[slot]] * weight).astype(jnp.bfloat16)

        loop(0, SLOTS, pick)
        loop(1, NY, lambda step: hand(side, step).start())

    def sum_columns(side):
        row, col, total = sides[side][2], sides[side][3], sides[side][4]
        loop(1, NY, lambda step: handed(side, step).wait_recv())

        def one(to):
            acc = row[my * NZ + to].astype(jnp.float32)
            for step in range(1, NY):
                acc = acc + col[lax.rem(my + step, NY), to].astype(jnp.float32)
            total[to] = acc.astype(jnp.bfloat16)

        def one_sent(step):
            to = lax.rem(mz + far_first(step), NZ)
            one(to)
            bring(side, to).start()

        loop(1, NZ, one_sent)
        one(mz)
        bring_own(side).start()

    sum_reads(0)
    sum_columns(0)
    sum_reads(1)
    sum_columns(1)

    for which in range(2):
        own(which).wait()
        loop(1, NH, lambda step: exchanged(which, lax.rem(mh + step, NH)).wait_recv())
        loop(1, NH, lambda step: exchange(which, lax.rem(mh + step, NH)).wait_send())
    for side in range(2):
        loop(1, NZ, lambda step: give(side, lax.rem(mz + step, NZ)).wait_send())
        loop(1, NY, lambda step: hand(side, step).wait_send())
        bring_own(side).wait()
        loop(1, NZ, lambda step: brought(side, lax.rem(mz + step, NZ)).wait_recv())
        loop(1, NZ, lambda step: bring(side, lax.rem(mz + step, NZ)).wait_send())


def give_back(order, same, last, has, attn, q_grad, k_part, v_part):
    any_spec = pl.BlockSpec(memory_space=pl.ANY)
    part = (TILES, BLOCK, D_HEAD)
    dma = pltpu.SemaphoreType.DMA
    bf16 = jnp.bfloat16
    return pl.pallas_call(
        give_kernel,
        out_shape=(
            jax.ShapeDtypeStruct((TEXT // NH, NH * WIDTH), bf16),
            jax.ShapeDtypeStruct((TEXT // NH, NH * WIDTH), bf16),
            jax.ShapeDtypeStruct((TILES, NZ, BLOCK, D_HEAD), bf16),
            jax.ShapeDtypeStruct((TILES, NZ, BLOCK, D_HEAD), bf16),
        ),
        in_specs=[pl.BlockSpec(memory_space=pltpu.SMEM)] * 4 + [any_spec] * 4,
        out_specs=(any_spec,) * 4,
        scratch_shapes=[
            pltpu.VMEM((NZ * READS,) + part, bf16),
            pltpu.VMEM((NZ * READS,) + part, bf16),
            pltpu.VMEM((NZ * READS,) + part, jnp.float32),
            pltpu.VMEM((SLOTS,) + part, bf16),
            pltpu.VMEM((SLOTS,) + part, bf16),
            pltpu.VMEM((NY, NZ) + part, bf16),
            pltpu.VMEM((NY, NZ) + part, bf16),
            pltpu.VMEM((NZ,) + part, bf16),
            pltpu.VMEM((NZ,) + part, bf16),
            dma((2, NH)), dma((2, NH)),
            dma((2, NZ)), dma((2, NZ)),
            dma((2, NY)), dma((2, NY)),
            dma((2, NZ)), dma((2, NZ)),
            dma((6,)),
        ],
        compiler_params=pltpu.CompilerParams(
            collective_id=2, has_side_effects=True, vmem_limit_bytes=VMEM_BYTES
        ),
        name="give_back",
    )(
        order, same, last, has,
        attn.reshape(NH, TEXT // NH, WIDTH), q_grad.reshape(NH, TEXT // NH, WIDTH),
        k_part.reshape((NZ * READS,) + part), v_part.reshape((NZ * READS,) + part),
    )


def on_device(
    queries, out_grad, keys, values, image_owner, tile_count, seq_images, text_len, tile_mask
):
    images = tile_count.shape[0]
    device_index = lax.axis_index("dp")
    matches = seq_images.reshape(-1)[:, None] == jnp.arange(images, dtype=jnp.int32)[None, :]
    slot_of = jnp.sum(jnp.where(matches, image_owner[None, :], 0), axis=1)
    counts = jnp.sum(jnp.where(matches, tile_count[None, :], 0), axis=1)

    my_counts = lax.dynamic_slice_in_dim(counts, device_index * READS, READS, 0)
    units = jnp.arange(UNITS, dtype=jnp.int32)
    tile_ok = (
        (jnp.arange(TILES, dtype=jnp.int32)[None, :] < my_counts[:, None]) & (tile_mask[0] == 1)
    ).reshape(-1)
    sort_key = jnp.where(tile_ok, units, units + UNITS)
    rank = jnp.sum((sort_key[None, :] < sort_key[:, None]).astype(jnp.int32), axis=1)
    unit_order = jnp.sum(jnp.where(rank[None, :] == units[:, None], units[None, :], 0), axis=1)
    facts = jnp.stack([jnp.sum(tile_ok.astype(jnp.int32)), text_len[0]])

    row_reads = NZ * READS
    row_slots = lax.dynamic_slice_in_dim(slot_of, device_index // NZ * row_reads, row_reads, 0)
    reads = jnp.arange(row_reads, dtype=jnp.int32)
    read_key = row_slots * row_reads + reads
    read_rank = jnp.sum((read_key[None, :] < read_key[:, None]).astype(jnp.int32), axis=1)
    placed = read_rank[None, :] == reads[:, None]
    read_order = jnp.sum(jnp.where(placed, reads[None, :], 0), axis=1)
    sorted_slots = jnp.sum(jnp.where(placed, row_slots[None, :], 0), axis=1)
    same = jnp.concatenate(
        [jnp.zeros((1,), jnp.int32), (sorted_slots[1:] == sorted_slots[:-1]).astype(jnp.int32)]
    )
    slot_ids = jnp.arange(SLOTS, dtype=jnp.int32)
    up_to = jnp.sum((row_slots[None, :] <= slot_ids[:, None]).astype(jnp.int32), axis=1)
    has = jnp.max((row_slots[None, :] == slot_ids[:, None]).astype(jnp.int32), axis=1)
    last = jnp.maximum(up_to - 1, 0)

    split = (TILES, NZ, BLOCK, D_HEAD)
    q_heads, g_heads, k_reads, v_reads = fetch(
        slot_of, queries[0], out_grad[0], keys.reshape(split), values.reshape(split)
    )
    attn, q_grad, k_part, v_part = attend(unit_order, facts, q_heads, g_heads, k_reads, v_reads)
    attn_out, query_grad, key_grad, value_grad = give_back(
        read_order, same, last, has, attn, q_grad, k_part, v_part
    )
    return (
        attn_out[None],
        query_grad[None],
        key_grad.reshape(keys.shape),
        value_grad.reshape(values.shape),
    )


def solution(mesh):
    in_specs = (
        P("dp", "heads", None),
        P("dp", "heads", None),
        P("dp", None, "heads"),
        P("dp", None, "heads"),
        P(),
        P(),
        P(),
        P("dp"),
        P("dp", None, None),
    )
    out_specs = (
        P("dp", "heads", None),
        P("dp", "heads", None),
        P("dp", None, "heads"),
        P("dp", None, "heads"),
    )
    return jax.shard_map(
        on_device, mesh=mesh, in_specs=in_specs, out_specs=out_specs, check_vma=False
    )
```
